32 devices in a mesh: row: 8 (over z, y), col: 4 (over x, core).
Axes of the slice: x: 2, y: 2, z: 4, core: 2. Of those that a mesh axis runs over, the one named last changes fastest.
Arguments:
- weights: float32 [192, 5, 256, 256], P(('row', 'col')), may hold values from 0.01 to 1
- band_mask: int32 [192, 5], P(('row', 'col')), may hold values from 0 to 1, as said below
- out_slots: int32 [192, 4], P(('row', 'col')), may hold values from -1 to 8, as said below
Outputs:
- flow: float32 [192, 4, 256, 256], P(('row', 'col'))
The draws below stay inside these ranges and needn't reach their ends.
Inputs may be any that keep to these rules, and one draw needn't show every extreme that they name: `band_mask`: the diagonal block (t = 2) is always 1; blocks whose column lies outside the matrix are 0. `out_slots`: in each row the live entries come first, are distinct, name block columns inside the matrix, and the first is 4; the rest are -1. Row 0 has all 4 slots live.
All inputs are finite; a program needn't handle non-finite values.
Results may differ from the reference program's by a relative error of at most 0.0003.
Values sent between devices are 32-bit elements; how exact they have to be, the bound alone decides.
A program may use at most 128 MiB of HBM per device.

```python
import math
import jax
import jax.numpy as jnp
from jax import lax

B = 256
W = 2
CAPO = 4
NBAND = 5
NB = 192


def draw_band_mask(key, part):
    row_ids = jnp.arange(NB, dtype=jnp.int32)[:, None]
    offsets = jnp.arange(NBAND, dtype=jnp.int32)[None, :]
    target = row_ids + offsets - W
    inside = (target >= 0) & (target < NB)
    coin_flips = jax.random.randint(key, (NB, NBAND), 0, 4)
    present = jnp.where(offsets == W, 1, jnp.where(inside & (coin_flips > 0), 1, 0))
    return present.astype(jnp.int32)


def draw_out_slots(key, part):
    key_scores = jax.random.fold_in(key, 11)
    key_full = jax.random.fold_in(key, 12)
    key_count = jax.random.fold_in(key, 13)
    row_ids = jnp.arange(NB, dtype=jnp.int32)[:, None]
    candidates = jnp.arange(4 * W + 1, dtype=jnp.int32)[None, :]
    target = row_ids + candidates - 2 * W
    usable = (target >= 0) & (target < NB) & (candidates != 2 * W)
    scores = jax.random.randint(key_scores, (NB, 4 * W + 1), 0, 65536) * (4 * W + 1) + candidates
    scores = jnp.where(usable, scores, scores + (1 << 28))
    ranking = jnp.argsort(scores, axis=1).astype(jnp.int32)
    chosen = ranking[:, :CAPO - 1]
    slot_ids = jnp.concatenate([jnp.full((NB, 1), 2 * W, jnp.int32), chosen], axis=1)
    full_rows = jax.random.randint(key_full, (NB,), 0, 2) == 0
    counts = jnp.where(full_rows, CAPO, jax.random.randint(key_count, (NB,), 1, CAPO + 1))
    counts = counts.at[0].set(CAPO)
    live_slot = jnp.arange(CAPO, dtype=jnp.int32)[None, :] < counts[:, None]
    return jnp.where(live_slot, slot_ids, -1).astype(jnp.int32)


def block_scale(own_key, dims, shards, low, top_value):
    gain, own = 1.0, jax.random.fold_in(own_key, 6)
    for axis_at, shards_of in shards:
        draws = jnp.exp(jax.random.uniform(jax.random.fold_in(own, axis_at), (shards_of,), jnp.float32, low / len(shards), top_value / len(shards)))
        gain = gain * jnp.repeat(draws, dims[axis_at] // shards_of).reshape([-1 if axis == axis_at else 1 for axis in range(len(dims))])
    return gain


def setup_inputs(seed: int = 0) -> dict:
    streams_of = jax.random.split(jax.random.key(seed), 4)
    return {
        "weights": jnp.clip(jnp.exp(math.log(1.0) - 4.6051702 * jax.random.uniform(streams_of[0], (NB, NBAND, B, B), jnp.float32) ** block_scale(streams_of[0], (NB, NBAND, B, B), ((0, 32),), -0.2, 0.2)), 0.01, 1.0),
        "band_mask": draw_band_mask(jax.random.fold_in(streams_of[3], 71), 0),
        "out_slots": draw_out_slots(jax.random.fold_in(streams_of[3], 71), 0),
    }


highest = lax.Precision.HIGHEST


def reference(weights, band_mask, out_slots):
    masked_weights = weights * band_mask.astype(jnp.float32)[:, :, None, None]
    padded_weights = jnp.pad(masked_weights, ((2 * W, 2 * W), (0, 0), (0, 0), (0, 0)))
    eye_block = jnp.eye(B, dtype=jnp.float32)
    identity_band = (jnp.arange(NBAND) == W).astype(jnp.float32)[:, None, None] * eye_block

    def symmetric_row(padded_index):
        window = lax.dynamic_slice_in_dim(padded_weights, padded_index, NBAND, 0)
        own_rows = window[W]
        mirrored = jnp.stack([window[offset, 2 * W - offset].T for offset in range(NBAND)])
        global_row = padded_index - W
        inside = ((global_row >= 0) & (global_row < NB)).astype(jnp.float32)
        return 0.5 * (own_rows + mirrored) + inside * identity_band

    symmetric_padded = lax.map(symmetric_row, jnp.arange(NB + 2 * W, dtype=jnp.int32))
    degree = jnp.sum(symmetric_padded, axis=(1, 3))
    padded_ids = jnp.arange(NB + 2 * W, dtype=jnp.int32) - W
    inside_rows = (padded_ids >= 0) & (padded_ids < NB)
    safe_degree = jnp.where(inside_rows[:, None], degree, jnp.float32(1.0))
    offsets = jnp.arange(NBAND, dtype=jnp.int32)

    def expand_row(row_id):
        slot_ids = out_slots[row_id]
        live_slot = slot_ids >= 0
        band_pick = slot_ids[:, None] - offsets[None, :]
        usable = live_slot[:, None] & (band_pick >= 0) & (band_pick <= 2 * W)
        picked = jnp.clip(band_pick, 0, 2 * W)
        source_rows = row_id + offsets
        right_rows = symmetric_padded[source_rows[None, :], picked] / safe_degree[source_rows][None, :, :, None]
        right_rows = right_rows * usable.astype(jnp.float32)[:, :, None, None]
        left_rows = symmetric_padded[row_id + W]
        expanded = jnp.einsum('tij,stjk->sik', left_rows, right_rows, precision=highest)
        return expanded * expanded

    inflated = lax.map(expand_row, jnp.arange(NB, dtype=jnp.int32))
    live_all = out_slots >= 0
    positions = jnp.arange(NB, dtype=jnp.int32)[:, None] + out_slots
    positions = jnp.where(live_all, positions, NB + 4 * W).astype(jnp.int32)
    block_sums = jnp.sum(inflated, axis=2) * live_all.astype(jnp.float32)[:, :, None]
    totals = jnp.zeros((NB + 4 * W + 1, B), jnp.float32).at[positions.reshape(-1)].add(block_sums.reshape(-1, B))
    slot_totals = totals[positions]
    safe_total = jnp.where(live_all[:, :, None], slot_totals, jnp.float32(1.0))
    return jnp.where(live_all[:, :, None, None], B * inflated / safe_total[:, :, None, :], jnp.float32(0.0))
```

```python
import functools

import jax
import jax.numpy as jnp
from jax import lax
from jax.experimental import pallas as pl
from jax.experimental.pallas import tpu as pltpu
from jax.sharding import PartitionSpec as P

B = 256
NBAND = 5
CAPO = 4
ROWS = 6
SLOTS = ROWS * CAPO
BLOCKS = ROWS * NBAND
COLS = 16
F32, BF16 = jnp.float32, jnp.bfloat16
MESH = pl.DeviceIdType.MESH
CROSS = ((1, 0, 5), (28, 29, 24))
LANDS = (0, 2, 1)
INNER = ((3, 4, 8, 9), (26, 25, 21, 20))
DIAG = ((2, 7), (27, 22))
HIGHEST = lax.Precision.HIGHEST


def split(x):
    high = x.astype(BF16)
    return high, (x - high.astype(F32)).astype(BF16)


def dot(a, b):
    return jnp.dot(a, b, preferred_element_type=F32)


def dot_nt(a, b):
    return lax.dot_general(a, b, (((1,), (1,)), ((), ())), preferred_element_type=F32)


def product(a, b, mul=dot):
    return mul(a[0], b[0]) + (mul(a[0], b[1]) + mul(a[1], b[0]))


def kernel(
    names, sizes,
    slots, w_hbm, maskf, pick, put,
    inflated, scale,
    w, right_h, right_l, left_h, left_l, extra, packed, w_in, m_in, m_h, m_l, lx_h, lx_l,
    dinv, d_out, d_in, sums, part, part_in, totals,
    load_sem, w_send, w_recv, m_send, m_recv, d_send, d_recv, p_send, p_recv,
):
    ncol = sizes[1]
    count = sizes[0] * sizes[1]
    me = lax.axis_index(names[0]) * ncol + lax.axis_index(names[1])

    def at(by):
        there = me + by
        return (lax.div(there, ncol), lax.rem(there, ncol))

    def exists(by):
        return (me + by >= 0) & (me + by < count)

    steps = (-1, 1)
    far = (-1, 1, -2, 2)

    loads = [
        pltpu.make_async_copy(w_hbm.at[pl.ds(lo, n)], w.at[pl.ds(lo, n)], load_sem.at[j])
        for j, (lo, n) in enumerate(((0, 2), (5, 1), (24, 1), (28, 2), (2, 3), (6, 18), (25, 3)))
    ]
    for copy in loads:
        copy.start()

    barrier = pltpu.get_barrier_semaphore()
    for by in far:

        @pl.when(exists(by))
        def _():
            pl.semaphore_signal(barrier, inc=1, device_id=at(by), device_id_type=MESH)

    for copy in loads[:4]:
        copy.wait()
    for j in (0, 1, 5, 24, 28, 29):
        w[j] = w[j] * maskf[j]

    peers = sum(exists(by).astype(jnp.int32) for by in far)
    pl.semaphore_wait(barrier, peers)

    def remote(src, dst, ssem, rsem, by):
        return pltpu.make_async_remote_copy(
            src_ref=src, dst_ref=dst, send_sem=ssem, recv_sem=rsem, device_id=at(by), device_id_type=MESH
        )

    def w_copy(side, a, land_side, land):
        return remote(
            w.at[CROSS[side][a]], w_in.at[land_side, land],
            w_send.at[side, a], w_recv.at[land_side, land], steps[side],
        )

    def m_copy(side, a, land_side):
        src = packed.at[side] if a == 0 else w.at[INNER[side][a - 1]]
        return remote(src, m_in.at[land_side, a], m_send.at[side, a], m_recv.at[land_side, a], steps[side])

    def d_copy(side, land_side):
        return remote(d_out.at[side], d_in.at[land_side], d_send.at[side], d_recv.at[land_side], steps[side])

    def p_copy(j, land):
        return remote(part, part_in.at[land], p_send.at[j], p_recv.at[land], far[j])

    for side in range(2):

        @pl.when(exists(steps[side]))
        def _():
            for a in range(3):
                w_copy(side, a, 1 - side, LANDS[a]).start()

    zero = jnp.zeros((B, B), F32)
    for side in range(2):

        @pl.when(jnp.logical_not(exists(steps[side])))
        def _():
            for a in range(3):
                w_in[side, a] = zero
            for a in range(5):
                m_in[side, a] = zero
            d_in[side] = jnp.ones((8, B), F32)

    for j in range(4):

        @pl.when(jnp.logical_not(exists(far[j])))
        def _():
            part_in[j] = jnp.zeros((COLS, B), F32)

    for copy in loads[4:]:
        copy.wait()

    rows = lax.broadcasted_iota(jnp.int32, (B, B), 0)
    cols = lax.broadcasted_iota(jnp.int32, (B, B), 1)
    eye = (rows == cols).astype(F32)

    def diagonal(n, carry):
        j = n * NBAND + 2
        x = w[j] * maskf[j]
        s = 0.5 * (x + x.T) + eye
        w[j] = s
        h, l = split(s)
        right_h[j], right_l[j] = h, l
        return carry

    lax.fori_loop(0, ROWS, diagonal, 0)

    def pair(step):
        def run(n, carry):
            j = n * NBAND + 2 + step
            i = (n + step) * NBAND + 2 - step
            s = 0.5 * (w[j] * maskf[j] + (w[i] * maskf[i]).T)
            w[j] = s
            h, l = split(s)
            right_h[j], right_l[j] = h, l
            s = s.T
            w[i] = s
            h, l = split(s)
            right_h[i], right_l[i] = h, l
            return carry

        return run

    lax.fori_loop(0, ROWS - 1, pair(1), 0)
    lax.fori_loop(0, ROWS - 2, pair(2), 0)

    for side in range(2):
        first = w[DIAG[side][0]]
        packed[side] = jnp.where(rows > cols, first, w[DIAG[side][1]])
        d_out[side, 2:3, :] = jnp.sum(first * eye, axis=0, keepdims=True)

        @pl.when(exists(steps[side]))
        def _():
            for a in range(5):
                m_copy(side, a, 1 - side).start()

    right_h[BLOCKS] = jnp.zeros((B, B), BF16)
    right_l[BLOCKS] = jnp.zeros((B, B), BF16)
    for j in (0, 1, 8, 9):
        dinv[j] = jnp.ones((8, B), F32)

    for side in range(2):

        @pl.when(exists(steps[side]))
        def _():
            for a in range(3):
                w_copy(side, a, side, a).wait_recv()
            for a in range(3):
                w_copy(side, a, 1 - side, LANDS[a]).wait_send()

        for a in range(3):
            j = CROSS[side][a]
            s = 0.5 * (w[j] + w_in[side, a].T)
            w[j] = s
            h, l = split(s)
            right_h[j], right_l[j] = h, l

    def degrees(n, carry):
        a = w[n * NBAND]
        for t in range(1, NBAND):
            a = a + w[n * NBAND + t]
        a = a[:, :128] + a[:, 128:]
        dinv[n + 2] = jnp.broadcast_to(1.0 / jnp.sum(a.T, axis=0, keepdims=True), (8, B))
        return carry

    lax.fori_loop(0, ROWS, degrees, 0)

    for side in range(2):
        for a in range(2):
            d_out[side, a : a + 1, :] = dinv[2 + a if side == 0 else 7 - a, 0:1, :]
        d_out[side, 3:8, :] = jnp.zeros((5, B), F32)

        @pl.when(exists(steps[side]))
        def _():
            d_copy(side, 1 - side).start()

    def scale_left(j, carry):
        n, t = lax.div(j, NBAND), lax.rem(j, NBAND)
        h, l = split(w[j] * dinv[n + t, 0:1, :])
        left_h[j], left_l[j] = h, l
        return carry

    lax.fori_loop(0, BLOCKS, scale_left, 0)

    def local(i, carry):
        n = lax.div(i, CAPO)
        u = slots[i]
        total = None
        for t in range(NBAND):
            k, v = n + t - 2, u - t
            usable = (k >= 0) & (k < ROWS) & (u >= 0) & (v >= 0) & (v < NBAND)
            r = jnp.where(usable, k * NBAND + v, BLOCKS)
            j = n * NBAND + t
            term = product((left_h[j], left_l[j]), (right_h[r], right_l[r]))
            total = term if total is None else total + term
        inflated[i] = total
        return carry

    lax.fori_loop(0, SLOTS, local, 0)

    crossing = []
    for side in range(2):

        @pl.when(exists(steps[side]))
        def _():
            d_copy(side, side).wait_recv()

        for a in range(3):
            row = (0, 1, 0)[a]
            h, l = split(w[CROSS[side][a]] * d_in[side, row : row + 1, :])
            lx_h[side, a], lx_l[side, a] = h, l
        base = side * 12
        lefts = [(lx_h.at[side, a], lx_l.at[side, a]) for a in range(3)]
        owns = [(right_h.at[j], right_l.at[j]) for j in CROSS[side]]

        def mul(a, b, how, lefts=lefts):
            return product((lefts[a][0][...], lefts[a][1][...]), (b[0][...], b[1][...]), how)

        extra[base + 4] = mul(0, owns[0], dot_nt) + mul(1, owns[1], dot_nt)
        extra[base + 5] = mul(0, owns[2], dot_nt)
        extra[base + 10] = mul(2, owns[0], dot_nt)
        extra[base + 11] = mul(2, owns[2], dot_nt)
        extra[base + 6] = zero
        crossing.append((base, mul))

    def arrived(side, a):
        @pl.when(exists(steps[side]))
        def _():
            m_copy(side, a, side).wait_recv()

    for side in range(2):
        base, mul = crossing[side]
        arrived(side, 0)
        m = m_in[side, 0]
        mt = m.T
        near = jnp.where(rows > cols, m, mt)
        near = jnp.where(rows == cols, d_in[side, 2:3, :], near)
        h, l = split(near)
        m_h[side, 0], m_l[side, 0] = h, l
        h, l = split(jnp.where(rows > cols, mt, m))
        m_h[side, 5], m_l[side, 5] = h, l
        ref = lambda a, side=side: (m_h.at[side, a], m_l.at[side, a])
        extra[base + 9] = mul(2, ref(0), dot)
        for a in range(1, 5):
            arrived(side, a)
            h, l = split(m_in[side, a])
            m_h[side, a], m_l[side, a] = h, l
            if a == 1:
                extra[base + 3] = mul(0, ref(0), dot) + mul(1, ref(1), dot_nt)
                extra[base + 2] = mul(0, ref(1), dot) + mul(1, ref(5), dot)
                extra[base + 8] = mul(2, ref(1), dot)
            if a == 2:
                extra[base + 7] = mul(2, ref(2), dot)
            if a == 3:
                extra[base + 1] = mul(0, ref(2), dot) + mul(1, ref(3), dot)
            if a == 4:
                extra[base] = mul(1, ref(4), dot)

    def finish(i, carry):
        n = lax.div(i, CAPO)
        u = slots[i]
        low = n < 2
        inner = (n < 2) | (n >= ROWS - 2)
        near_row = jnp.where(low, n, ROWS - 1 - n)
        c = n + u - 4
        near_col = jnp.where(low, c, ROWS - 1 - c) + 4
        usable = inner & (u >= 0) & (near_col >= 0) & (near_col < 6)
        x = jnp.where(usable, jnp.where(low, 0, 12) + near_row * 6 + near_col, 6)
        y = inflated[i] + extra[x]
        y = y * y
        inflated[i] = y
        sums[pl.ds(i, 1), :] = jnp.sum(y, axis=0, keepdims=True)
        return carry

    lax.fori_loop(0, SLOTS, finish, 0)

    part[...] = jnp.dot(put[...], sums[...], precision=HIGHEST, preferred_element_type=F32)
    mirror = (1, 0, 3, 2)
    for j in range(4):

        @pl.when(exists(far[j]))
        def _():
            p_copy(j, mirror[j]).start()

    totals[...] = part[...]
    for j in range(4):

        @pl.when(exists(far[j]))
        def _():
            p_copy(j, j).wait_recv()

    totals[0:8, :] += part_in[0, 6:14, :]
    totals[6:14, :] += part_in[1, 0:8, :]
    totals[0:2, :] += part_in[2, 12:14, :]
    totals[12:14, :] += part_in[3, 0:2, :]
    chosen = pick[...]
    slot_totals = jnp.dot(chosen, totals[...], precision=HIGHEST, preferred_element_type=F32)
    live = jnp.sum(chosen, axis=1, keepdims=True) > 0.5
    scale[...] = jnp.where(live, B / jnp.where(live, slot_totals, 1.0), 0.0)

    for side in range(2):

        @pl.when(exists(steps[side]))
        def _():
            for a in range(5):
                m_copy(side, a, 1 - side).wait_send()
            d_copy(side, 1 - side).wait_send()

    for j in range(4):

        @pl.when(exists(far[j]))
        def _():
            p_copy(j, mirror[j]).wait_send()


def normalise(x, scale, out):
    for s in range(CAPO):
        out[s] = x[s] * scale[0, s : s + 1, :]


def body(names, sizes, weights, band_mask, out_slots):
    maskf = jnp.broadcast_to(band_mask.astype(F32).reshape(BLOCKS, 1, 1), (BLOCKS, 1, B))
    slots = out_slots.reshape(SLOTS)
    position = (jnp.arange(ROWS, dtype=jnp.int32)[:, None] + out_slots).reshape(SLOTS)
    columns = jnp.arange(COLS, dtype=jnp.int32)
    pick = ((position[:, None] == columns) & (slots[:, None] >= 0)).astype(F32)
    vmem = pl.BlockSpec(memory_space=pltpu.VMEM)
    dma = pltpu.SemaphoreType.DMA
    inflated, scale = pl.pallas_call(
        functools.partial(kernel, names, sizes),
        out_shape=(
            jax.ShapeDtypeStruct((SLOTS, B, B), F32),
            jax.ShapeDtypeStruct((SLOTS, B), F32),
        ),
        in_specs=[pl.BlockSpec(memory_space=pltpu.SMEM), pl.BlockSpec(memory_space=pl.ANY), vmem, vmem, vmem],
        out_specs=(vmem, vmem),
        scratch_shapes=[
            pltpu.VMEM((BLOCKS, B, B), F32),
            pltpu.VMEM((BLOCKS + 1, B, B), BF16),
            pltpu.VMEM((BLOCKS + 1, B, B), BF16),
            pltpu.VMEM((BLOCKS, B, B), BF16),
            pltpu.VMEM((BLOCKS, B, B), BF16),
            pltpu.VMEM((24, B, B), F32),
            pltpu.VMEM((2, B, B), F32),
            pltpu.VMEM((2, 3, B, B), F32),
            pltpu.VMEM((2, 5, B, B), F32),
            pltpu.VMEM((2, 6, B, B), BF16),
            pltpu.VMEM((2, 6, B, B), BF16),
            pltpu.VMEM((2, 3, B, B), BF16),
            pltpu.VMEM((2, 3, B, B), BF16),
            pltpu.VMEM((10, 8, B), F32),
            pltpu.VMEM((2, 8, B), F32),
            pltpu.VMEM((2, 8, B), F32),
            pltpu.VMEM((SLOTS, B), F32),
            pltpu.VMEM((COLS, B), F32),
            pltpu.VMEM((4, COLS, B), F32),
            pltpu.VMEM((COLS, B), F32),
            dma((7,)),
            dma((2, 3)),
            dma((2, 3)),
            dma((2, 5)),
            dma((2, 5)),
            dma((2,)),
            dma((2,)),
            dma((4,)),
            dma((4,)),
        ],
        compiler_params=pltpu.CompilerParams(
            collective_id=0, has_side_effects=True, vmem_limit_bytes=56 * 1024 * 1024
        ),
    )(slots, weights.reshape(BLOCKS, B, B), maskf, pick, pick.T)
    flow = pl.pallas_call(
        normalise,
        out_shape=jax.ShapeDtypeStruct((SLOTS, B, B), F32),
        grid=(ROWS,),
        in_specs=[
            pl.BlockSpec((CAPO, B, B), lambda i: (i, 0, 0)),
            pl.BlockSpec((1, CAPO, B), lambda i: (i, 0, 0)),
        ],
        out_specs=pl.BlockSpec((CAPO, B, B), lambda i: (i, 0, 0)),
    )(inflated, scale.reshape(ROWS, CAPO, B))
    return flow.reshape(ROWS, CAPO, B, B)


def solution(mesh):
    names = tuple(mesh.axis_names)
    sizes = tuple(mesh.shape[name] for name in names)
    return jax.shard_map(
        functools.partial(body, names, sizes),
        mesh=mesh,
        in_specs=(
            P(("row", "col"), None, None, None),
            P(("row", "col"), None),
            P(("row", "col"), None),
        ),
        out_specs=P(("row", "col"), None, None, None),
        check_vma=False,
    )
```

```python
import functools

import jax
import jax.numpy as jnp
from jax import lax
from jax.experimental import pallas as pl
from jax.experimental.pallas import tpu as pltpu
from jax.sharding import PartitionSpec as P

B = 256
NBAND = 5
CAPO = 4
ROWS = 6
SLOTS = ROWS * CAPO
BLOCKS = ROWS * NBAND
COLS = 16
F32, BF16 = jnp.float32, jnp.bfloat16
MESH = pl.DeviceIdType.MESH
CROSS = ((1, 0, 5), (28, 29, 24))
LANDS = (0, 2, 1)
INNER = ((3, 4, 8, 9), (26, 25, 21, 20))
DIAG = ((2, 7), (27, 22))


def split(x):
    high = x.astype(BF16)
    return high, (x - high.astype(F32)).astype(BF16)


def dot(a, b):
    return jnp.dot(a, b, preferred_element_type=F32)


def dot_nt(a, b):
    return lax.dot_general(a, b, (((1,), (1,)), ((), ())), preferred_element_type=F32)


def product(a, b, mul=dot):
    return mul(a[0], b[0]) + (mul(a[0], b[1]) + mul(a[1], b[0]))


def kernel(
    names, sizes,
    slots, mask, w_hbm,
    inflated, scale,
    w, right_h, right_l, left_h, left_l, extra, packed, w_in, m_in, m_h, m_l, lx_h, lx_l,
    dinv, d_out, d_in, part, part_in, totals,
    load_sem, w_send, w_recv, m_send, m_recv, d_send, d_recv, p_send, p_recv,
):
    ncol = sizes[1]
    count = sizes[0] * sizes[1]
    me = lax.axis_index(names[0]) * ncol + lax.axis_index(names[1])

    def at(by):
        there = me + by
        return (lax.div(there, ncol), lax.rem(there, ncol))

    def exists(by):
        return (me + by >= 0) & (me + by < count)

    steps = (-1, 1)
    far = (-1, 1, -2, 2)

    loads = [
        pltpu.make_async_copy(w_hbm.at[pl.ds(lo, n)], w.at[pl.ds(lo, n)], load_sem.at[j])
        for j, (lo, n) in enumerate(((0, 2), (5, 1), (24, 1), (28, 2), (2, 3), (6, 18), (25, 3)))
    ]
    for copy in loads:
        copy.start()

    barrier = pltpu.get_barrier_semaphore()
    for by in far:

        @pl.when(exists(by))
        def _():
            pl.semaphore_signal(barrier, inc=1, device_id=at(by), device_id_type=MESH)

    for copy in loads[:4]:
        copy.wait()
    for j in (0, 1, 5, 24, 28, 29):
        w[j] = w[j] * mask[j // NBAND, j % NBAND].astype(F32)

    peers = sum(exists(by).astype(jnp.int32) for by in far)
    pl.semaphore_wait(barrier, peers)

    def remote(src, dst, ssem, rsem, by):
        return pltpu.make_async_remote_copy(
            src_ref=src, dst_ref=dst, send_sem=ssem, recv_sem=rsem, device_id=at(by), device_id_type=MESH
        )

    def w_copy(side, a, land_side, land):
        return remote(
            w.at[CROSS[side][a]], w_in.at[land_side, land],
            w_send.at[side, a], w_recv.at[land_side, land], steps[side],
        )

    def m_copy(side, a, land_side):
        src = packed.at[side] if a == 0 else w.at[INNER[side][a - 1]]
        return remote(src, m_in.at[land_side, a], m_send.at[side, a], m_recv.at[land_side, a], steps[side])

    def d_copy(side, land_side):
        return remote(d_out.at[side], d_in.at[land_side], d_send.at[side], d_recv.at[land_side], steps[side])

    def p_copy(j, land):
        return remote(part, part_in.at[land], p_send.at[j], p_recv.at[land], far[j])

    for side in range(2):

        @pl.when(exists(steps[side]))
        def _():
            for a in range(3):
                w_copy(side, a, 1 - side, LANDS[a]).start()

    zero = jnp.zeros((B, B), F32)
    for side in range(2):

        @pl.when(jnp.logical_not(exists(steps[side])))
        def _():
            for a in range(3):
                w_in[side, a] = zero
            for a in range(5):
                m_in[side, a] = zero
            d_in[side] = jnp.ones((8, B), F32)

    for j in range(4):

        @pl.when(jnp.logical_not(exists(far[j])))
        def _():
            part_in[j] = jnp.zeros((COLS, B), F32)

    for copy in loads[4:]:
        copy.wait()

    rows = lax.broadcasted_iota(jnp.int32, (B, B), 0)
    cols = lax.broadcasted_iota(jnp.int32, (B, B), 1)
    eye = (rows == cols).astype(F32)

    def diagonal(n, carry):
        j = n * NBAND + 2
        x = w[j] * mask[n, 2].astype(F32)
        s = 0.5 * (x + x.T) + eye
        w[j] = s
        h, l = split(s)
        right_h[j], right_l[j] = h, l
        return carry

    lax.fori_loop(0, ROWS, diagonal, 0)

    def pair(step):
        def run(n, carry):
            j = n * NBAND + 2 + step
            i = (n + step) * NBAND + 2 - step
            upper = w[j] * mask[n, 2 + step].astype(F32)
            s = 0.5 * (upper + (w[i] * mask[n + step, 2 - step].astype(F32)).T)
            w[j] = s
            h, l = split(s)
            right_h[j], right_l[j] = h, l
            s = s.T
            w[i] = s
            h, l = split(s)
            right_h[i], right_l[i] = h, l
            return carry

        return run

    lax.fori_loop(0, ROWS - 1, pair(1), 0)
    lax.fori_loop(0, ROWS - 2, pair(2), 0)

    for side in range(2):
        first = w[DIAG[side][0]]
        packed[side] = jnp.where(rows > cols, first, w[DIAG[side][1]])
        d_out[side, 2:3, :] = jnp.sum(first * eye, axis=0, keepdims=True)

        @pl.when(exists(steps[side]))
        def _():
            for a in range(5):
                m_copy(side, a, 1 - side).start()

    right_h[BLOCKS] = jnp.zeros((B, B), BF16)
    right_l[BLOCKS] = jnp.zeros((B, B), BF16)
    for j in (0, 1, 8, 9):
        dinv[j] = jnp.ones((8, B), F32)

    for side in range(2):

        @pl.when(exists(steps[side]))
        def _():
            for a in range(3):
                w_copy(side, a, side, a).wait_recv()
            for a in range(3):
                w_copy(side, a, 1 - side, LANDS[a]).wait_send()

        for a in range(3):
            j = CROSS[side][a]
            s = 0.5 * (w[j] + w_in[side, a].T)
            w[j] = s
            h, l = split(s)
            right_h[j], right_l[j] = h, l

    def degrees(n, carry):
        a = w[n * NBAND]
        for t in range(1, NBAND):
            a = a + w[n * NBAND + t]
        a = a[:, :128] + a[:, 128:]
        dinv[n + 2] = jnp.broadcast_to(1.0 / jnp.sum(a.T, axis=0, keepdims=True), (8, B))
        return carry

    lax.fori_loop(0, ROWS, degrees, 0)

    for side in range(2):
        for a in range(2):
            d_out[side, a : a + 1, :] = dinv[2 + a if side == 0 else 7 - a, 0:1, :]
        d_out[side, 3:8, :] = jnp.zeros((5, B), F32)

        @pl.when(exists(steps[side]))
        def _():
            d_copy(side, 1 - side).start()

    def scale_left(j, carry):
        n, t = lax.div(j, NBAND), lax.rem(j, NBAND)
        h, l = split(w[j] * dinv[n + t, 0:1, :])
        left_h[j], left_l[j] = h, l
        return carry

    lax.fori_loop(0, BLOCKS, scale_left, 0)

    def term(n, t, u, live):
        v = u - t
        r = jnp.where(live & (v >= 0) & (v < NBAND), (n + t - 2) * NBAND + v, BLOCKS)
        j = n * NBAND + t
        return product((left_h[j], left_l[j]), (right_h[r], right_l[r]))

    def end_rows(i, carry):
        n = jnp.where(i < CAPO, 0, ROWS - 1)
        s = lax.rem(i, CAPO)
        u = slots[n, s]
        first = jnp.where(i < CAPO, 2, 0)
        total = term(n, first, u, u >= 0)
        for t in range(1, 3):
            total = total + term(n, first + t, u, u >= 0)
        inflated[n * CAPO + s] = total
        return carry

    def middle_rows(i, carry):
        n, s = lax.div(i, CAPO), lax.rem(i, CAPO)
        u = slots[n, s]
        first = jnp.where(n == 1, 1, jnp.where(n == 4, 0, (u > 4).astype(jnp.int32)))
        total = term(n, first, u, u >= 0)
        for t in range(1, 4):
            total = total + term(n, first + t, u, u >= 0)
        inflated[i] = total
        return carry

    def last_terms(n, carry):
        inflated[n * CAPO] += term(n, 4, 4, True)
        return carry

    lax.fori_loop(0, 2 * CAPO, end_rows, 0)
    lax.fori_loop(CAPO, SLOTS - CAPO, middle_rows, 0)
    lax.fori_loop(2, 4, last_terms, 0)

    crossing = []
    for side in range(2):

        @pl.when(exists(steps[side]))
        def _():
            d_copy(side, side).wait_recv()

        for a in range(3):
            row = (0, 1, 0)[a]
            h, l = split(w[CROSS[side][a]] * d_in[side, row : row + 1, :])
            lx_h[side, a], lx_l[side, a] = h, l
        base = side * 12
        lefts = [(lx_h.at[side, a], lx_l.at[side, a]) for a in range(3)]
        owns = [(right_h.at[j], right_l.at[j]) for j in CROSS[side]]

        def mul(a, b, how, lefts=lefts):
            return product((lefts[a][0][...], lefts[a][1][...]), (b[0][...], b[1][...]), how)

        extra[base + 4] = mul(0, owns[0], dot_nt) + mul(1, owns[1], dot_nt)
        extra[base + 5] = mul(0, owns[2], dot_nt)
        extra[base + 10] = mul(2, owns[0], dot_nt)
        extra[base + 11] = mul(2, owns[2], dot_nt)
        extra[base + 6] = zero
        crossing.append((base, mul))

    def arrived(side, a):
        @pl.when(exists(steps[side]))
        def _():
            m_copy(side, a, side).wait_recv()

    for side in range(2):
        base, mul = crossing[side]
        arrived(side, 0)
        m = m_in[side, 0]
        mt = m.T
        near = jnp.where(rows > cols, m, mt)
        near = jnp.where(rows == cols, d_in[side, 2:3, :], near)
        h, l = split(near)
        m_h[side, 0], m_l[side, 0] = h, l
        h, l = split(jnp.where(rows > cols, mt, m))
        m_h[side, 5], m_l[side, 5] = h, l
        ref = lambda a, side=side: (m_h.at[side, a], m_l.at[side, a])
        extra[base + 9] = mul(2, ref(0), dot)
        for a in range(1, 5):
            arrived(side, a)
            h, l = split(m_in[side, a])
            m_h[side, a], m_l[side, a] = h, l
            if a == 1:
                extra[base + 3] = mul(0, ref(0), dot) + mul(1, ref(1), dot_nt)
                extra[base + 2] = mul(0, ref(1), dot) + mul(1, ref(5), dot)
                extra[base + 8] = mul(2, ref(1), dot)
            if a == 2:
                extra[base + 7] = mul(2, ref(2), dot)
            if a == 3:
                extra[base + 1] = mul(0, ref(2), dot) + mul(1, ref(3), dot)
            if a == 4:
                extra[base] = mul(1, ref(4), dot)

    lines = lax.broadcasted_iota(jnp.int32, (COLS, B), 0)
    part[...] = jnp.zeros((COLS, B), F32)

    def finish(i, carry):
        n = lax.div(i, CAPO)
        u = slots[n, lax.rem(i, CAPO)]
        low = n < 2
        inner = (n < 2) | (n >= ROWS - 2)
        near_row = jnp.where(low, n, ROWS - 1 - n)
        c = n + u - 4
        near_col = jnp.where(low, c, ROWS - 1 - c) + 4
        usable = inner & (u >= 0) & (near_col >= 0) & (near_col < 6)
        x = jnp.where(usable, jnp.where(low, 0, 12) + near_row * 6 + near_col, 6)
        y = inflated[i] + extra[x]
        y = y * y
        inflated[i] = y
        here = (lines == n + u) & (u >= 0)
        part[...] += jnp.where(here, jnp.sum(y, axis=0, keepdims=True), 0.0)
        return carry

    lax.fori_loop(0, SLOTS, finish, 0)

    mirror = (1, 0, 3, 2)
    for j in range(4):

        @pl.when(exists(far[j]))
        def _():
            p_copy(j, mirror[j]).start()

    totals[...] = part[...]
    for j in range(4):

        @pl.when(exists(far[j]))
        def _():
            p_copy(j, j).wait_recv()

    totals[0:8, :] += part_in[0, 6:14, :]
    totals[6:14, :] += part_in[1, 0:8, :]
    totals[0:2, :] += part_in[2, 12:14, :]
    totals[12:14, :] += part_in[3, 0:2, :]
    everything = totals[...]

    for i in range(SLOTS):
        u = slots[i // CAPO, i % CAPO]
        mine = jnp.sum(jnp.where(lines == i // CAPO + u, everything, 0.0), axis=0, keepdims=True)
        scale[i : i + 1, :] = jnp.where(u >= 0, B / jnp.where(u >= 0, mine, 1.0), 0.0)

    for side in range(2):

        @pl.when(exists(steps[side]))
        def _():
            for a in range(5):
                m_copy(side, a, 1 - side).wait_send()
            d_copy(side, 1 - side).wait_send()

    for j in range(4):

        @pl.when(exists(far[j]))
        def _():
            p_copy(j, mirror[j]).wait_send()


def normalise(x, scale, flow, out, sems):
    copies = []
    for n in range(ROWS):
        for j in range(n * CAPO, (n + 1) * CAPO):
            out[j] = x[j] * scale[j : j + 1, :]
        rows = pl.ds(n * CAPO, CAPO)
        copy = pltpu.make_async_copy(out.at[rows], flow.at[rows], sems.at[n])
        copy.start()
        copies.append(copy)
    for copy in copies:
        copy.wait()


def body(names, sizes, weights, band_mask, out_slots):
    vmem = pl.BlockSpec(memory_space=pltpu.VMEM)
    dma = pltpu.SemaphoreType.DMA
    inflated, scale = pl.pallas_call(
        functools.partial(kernel, names, sizes),
        out_shape=(
            pltpu.VMEM((SLOTS, B, B), F32),
            pltpu.VMEM((SLOTS, B), F32),
        ),
        in_specs=[
            pl.BlockSpec(memory_space=pltpu.SMEM),
            pl.BlockSpec(memory_space=pltpu.SMEM),
            pl.BlockSpec(memory_space=pl.ANY),
        ],
        out_specs=(vmem, vmem),
        scratch_shapes=[
            pltpu.VMEM((BLOCKS, B, B), F32),
            pltpu.VMEM((BLOCKS + 1, B, B), BF16),
            pltpu.VMEM((BLOCKS + 1, B, B), BF16),
            pltpu.VMEM((BLOCKS, B, B), BF16),
            pltpu.VMEM((BLOCKS, B, B), BF16),
            pltpu.VMEM((24, B, B), F32),
            pltpu.VMEM((2, B, B), F32),
            pltpu.VMEM((2, 3, B, B), F32),
            pltpu.VMEM((2, 5, B, B), F32),
            pltpu.VMEM((2, 6, B, B), BF16),
            pltpu.VMEM((2, 6, B, B), BF16),
            pltpu.VMEM((2, 3, B, B), BF16),
            pltpu.VMEM((2, 3, B, B), BF16),
            pltpu.VMEM((10, 8, B), F32),
            pltpu.VMEM((2, 8, B), F32),
            pltpu.VMEM((2, 8, B), F32),
            pltpu.VMEM((COLS, B), F32),
            pltpu.VMEM((4, COLS, B), F32),
            pltpu.VMEM((COLS, B), F32),
            dma((7,)),
            dma((2, 3)),
            dma((2, 3)),
            dma((2, 5)),
            dma((2, 5)),
            dma((2,)),
            dma((2,)),
            dma((4,)),
            dma((4,)),
        ],
        compiler_params=pltpu.CompilerParams(
            collective_id=0, has_side_effects=True, vmem_limit_bytes=46 * 1024 * 1024
        ),
    )(out_slots, band_mask, weights.reshape(BLOCKS, B, B))
    flow = pl.pallas_call(
        normalise,
        out_shape=jax.ShapeDtypeStruct((SLOTS, B, B), F32),
        in_specs=[vmem, vmem],
        out_specs=pl.BlockSpec(memory_space=pl.ANY),
        scratch_shapes=[pltpu.VMEM((SLOTS, B, B), F32), dma((ROWS,))],
        compiler_params=pltpu.CompilerParams(vmem_limit_bytes=20 * 1024 * 1024),
    )(inflated, scale)
    return flow.reshape(ROWS, CAPO, B, B)


def solution(mesh):
    names = tuple(mesh.axis_names)
    sizes = tuple(mesh.shape[name] for name in names)
    return jax.shard_map(
        functools.partial(body, names, sizes),
        mesh=mesh,
        in_specs=(
            P(("row", "col"), None, None, None),
            P(("row", "col"), None),
            P(("row", "col"), None),
        ),
        out_specs=P(("row", "col"), None, None, None),
        check_vma=False,
    )
```
